768 devices in a mesh: src: 32 (over y, z_lo), dst: 24 (over x, z_hi, core).
Axes of the slice: x: 4, y: 8, z: 12 (z_hi: 3, z_lo: 4; z = z_hi * 4 + z_lo), core: 2. Of those that a mesh axis runs over, the one named last changes fastest.
Arguments:
- prior: float32 [98304, 256], P(('src', 'dst')), may hold values from -6 to 6
- degrees: int32 [98304], P(('src', 'dst')), may hold values from 1 to 15360, as said below
- seed_mask: int32 [98304], P(('src', 'dst')), may hold values 0 or 1
- seed_labels: int32 [98304], P(('src', 'dst')), may hold values from 0 to 255
- adjacency: bfloat16 [32, 24, 24, 5, 128, 128], P('src', 'dst'), may hold values from 0 to 1, as said below
- block_cols: int32 [32, 24, 24, 5], P('src', 'dst'), may hold values from 0 to 31
- slot_counts: int32 [32, 24, 24], P('src', 'dst'), may hold values from 1 to 5, as said below
Outputs:
- scores: float32 [98304, 256], P(('src', 'dst'))
The draws below stay inside these ranges and needn't reach their ends.
Inputs may be any that keep to these rules, and one draw needn't show every extreme that they name: `slot_counts`: each device holds at most 5 live slots in a row block; local row block 0 of row group 0 has exactly 5 on every device. `block_cols`: local column indices within one column group. `adjacency`: entries are 0 or 1. degrees[n] is the number of ones in node n's row of the adjacency, over the live slots of all devices; some node reaches the most.
All inputs are finite; a program needn't handle non-finite values. No bound on the sum of `seed_mask` on one device may be relied on, other than what follows from the above.
Results may differ from the reference program's by a relative error of at most 0.005.
Values may be sent and summed in bfloat16 or wider, within the bound.
No kernel may reach another device: no remote copies, remote signals or barrier semaphores. Data moves between devices by JAX's collectives and lax.ppermute only.
A program may use at most 32 MiB of HBM per device.

```python
import jax
import jax.numpy as jnp
from jax import lax

C = 256
BLK = 128
PB = 1
S = 5
SWEEPS = 2
ROWBLK = 24
NODES = 98304
N_SRC = 32
N_DST = 24


def draw_slot_counts(key, part):
    key = jax.random.fold_in(key, 23)
    first, second, third = jax.random.split(key, 3)
    shape = (N_SRC, N_DST, ROWBLK)
    ceiling = jax.random.randint(first, (N_SRC, N_DST, 1), 1, S + 1)
    raw_bits = jax.random.randint(second, shape, 0, 1048576)
    counts = 1 + raw_bits % ceiling
    chosen = jax.random.randint(third, (), 0, N_SRC * N_DST * ROWBLK)
    flat_index = jnp.arange(N_SRC * N_DST * ROWBLK, dtype=jnp.int32).reshape(shape)
    counts = jnp.where(flat_index == chosen, S, counts)
    src_ids = jnp.arange(N_SRC, dtype=jnp.int32).reshape(N_SRC, 1, 1)
    row_blocks = jnp.arange(ROWBLK, dtype=jnp.int32).reshape(1, 1, ROWBLK)
    counts = jnp.where((src_ids == 0) & (row_blocks == 0), S, counts)
    return counts.astype(jnp.int32)


def edge_pattern(key):
    counts = draw_slot_counts(key, 0)
    inner = jax.random.fold_in(key, 37)
    first, second = jax.random.split(inner, 2)
    shape = (N_SRC, N_DST, ROWBLK, S, BLK, BLK)
    target = jax.random.randint(first, (N_SRC, 1, ROWBLK, 1, BLK, 1), 4, 65)
    raw_bits = jax.random.randint(second, shape, 0, 65536)
    edges = raw_bits * (N_DST * S * BLK) < 2 * target * 65536
    src_ids = jnp.arange(N_SRC, dtype=jnp.int32).reshape(N_SRC, 1, 1, 1, 1, 1)
    dst_ids = jnp.arange(N_DST, dtype=jnp.int32).reshape(1, N_DST, 1, 1, 1, 1)
    block_ids = jnp.arange(ROWBLK, dtype=jnp.int32).reshape(1, 1, ROWBLK, 1, 1, 1)
    slot_ids = jnp.arange(S, dtype=jnp.int32).reshape(1, 1, 1, S, 1, 1)
    row_ids = jnp.arange(BLK, dtype=jnp.int32).reshape(1, 1, 1, 1, BLK, 1)
    col_ids = jnp.arange(BLK, dtype=jnp.int32).reshape(1, 1, 1, 1, 1, BLK)
    forced = (dst_ids == 0) & (slot_ids == 0) & (row_ids == col_ids)
    dense_row = (src_ids == 0) & (block_ids == 0) & (row_ids == 0) & (col_ids >= 0)
    edges = edges | forced | dense_row
    live = slot_ids < counts[:, :, :, None, None, None]
    return (edges, live)


def draw_adjacency(key, part):
    edges, live = edge_pattern(key)
    return edges.astype(jnp.float32).astype(jnp.bfloat16)


def draw_degrees(key, part):
    edges, live = edge_pattern(key)
    counted = (edges & live).astype(jnp.int32)
    totals = jnp.sum(counted, axis=(1, 3, 5))
    return totals.reshape(N_SRC * ROWBLK * BLK).astype(jnp.int32)


def plant(drawn, key, least, largest):
    longest = drawn.shape.index(max(drawn.shape))
    spots = []
    for shift in (0, 1):
        where = [jax.random.randint(jax.random.fold_in(key, axis), (), 0, length) for axis, length in enumerate(drawn.shape)]
        where[longest] = (where[longest] + shift) % drawn.shape[longest]
        spots.append(tuple(where))
    return drawn.at[spots[0]].set(least).at[spots[1]].set(largest)


def block_levels(own_key, shape, cuts, least, largest):
    def one(axis_at, shards_of):
        steps = jax.random.uniform(jax.random.fold_in(jax.random.fold_in(own_key, 6), axis_at), (shards_of,), jnp.float32, least / len(cuts), largest / len(cuts))
        return jnp.repeat(jnp.exp(steps), shape[axis_at] // shards_of).reshape((-1,) + (1,) * (len(shape) - axis_at - 1))

    level = one(*cuts[0])
    for cut in cuts[1:]:
        level = level * one(*cut)
    return level


def scatter_about(own_key, shape, deviation, most, shards=(), held_as=jnp.bfloat16):
    loudness = block_levels(own_key, shape, shards, -0.22, 0.18) if shards else 1.0
    values = jax.random.normal(own_key, shape, jnp.float32) * deviation * loudness
    return jnp.minimum(jnp.maximum(values, -most), most).astype(held_as)


def setup_inputs(seed: int = 0) -> dict:
    streams_of = jax.random.split(jax.random.key(seed), 8)
    return {
        "prior": scatter_about(streams_of[0], (NODES, C), 1.0, 6.0, ((0, 768),), jnp.float32),
        "degrees": draw_degrees(jax.random.fold_in(streams_of[7], 71), 0),
        "seed_mask": plant((jax.random.randint(streams_of[2], (NODES,), 0, 8) < 1).astype(jnp.int32), jax.random.fold_in(streams_of[2], 1), 0, 1),
        "seed_labels": plant(jax.random.randint(streams_of[3], (NODES,), 0, C), jax.random.fold_in(streams_of[3], 1), 0, C - 1).astype(jnp.int32),
        "adjacency": draw_adjacency(jax.random.fold_in(streams_of[7], 71), 0),
        "block_cols": plant(jax.random.randint(streams_of[5], (N_SRC, N_DST, ROWBLK, S), 0, N_SRC * PB), jax.random.fold_in(streams_of[5], 1), 0, (N_SRC * PB) - 1).astype(jnp.int32),
        "slot_counts": draw_slot_counts(jax.random.fold_in(streams_of[7], 71), 0),
    }


RETAIN = 0.8

def reference(prior, degrees, seed_mask, seed_labels, adjacency, block_cols, slot_counts):
    inverse_root = lax.rsqrt(degrees.astype(jnp.float32))[:, None]
    classes = prior.shape[1]
    onehot = (seed_labels[:, None] == jnp.arange(classes, dtype=jnp.int32)[None, :]).astype(jnp.float32)
    seeded = seed_mask[:, None] > 0
    dst_ids = jnp.arange(N_DST, dtype=jnp.int32)
    slot_ids = jnp.arange(S, dtype=jnp.int32)
    scores = prior
    for sweep_index in range(SWEEPS):
        outgoing = (inverse_root * scores).astype(jnp.bfloat16)
        blocks = outgoing.reshape(N_SRC * N_DST * PB, BLK, classes)

        def row_group(inputs):
            group_adj, group_cols, group_counts = inputs

            def add_device(accum, item):
                weights, columns, counts, dst_id = item
                global_cols = (columns // PB * N_DST + dst_id) * PB + columns % PB
                picked = jnp.take(blocks, global_cols.astype(jnp.int32), axis=0).astype(jnp.float32)
                active = (slot_ids[None, :] < counts[:, None]).astype(jnp.float32)
                picked = picked * active[:, :, None, None]
                partial_value = jnp.einsum('rsij,rsjc->ric', weights.astype(jnp.float32), picked)
                partial_value = partial_value.reshape(ROWBLK * BLK, classes).astype(jnp.bfloat16).astype(jnp.float32)
                return (accum + partial_value, None)
            start = jnp.zeros((ROWBLK * BLK, classes), jnp.float32)
            totals, unused = lax.scan(add_device, start, (group_adj, group_cols, group_counts, dst_ids))
            return totals
        summed = lax.map(row_group, (adjacency, block_cols, slot_counts)).reshape(NODES, classes)
        hidden = RETAIN * inverse_root * summed + (1.0 - RETAIN) * prior
        scores = jnp.where(seeded, onehot, hidden)
    return scores
```

```python
import jax
import jax.numpy as jnp
from jax import lax
from jax.experimental import pallas as pl
from jax.experimental.pallas import tpu as pltpu
from jax.sharding import PartitionSpec as P

SWEEPS = 2
RETAIN = 0.8

Y, ZL, X, ZH, CORES = 8, 4, 4, 3, 2
PAIRS = X * ZH
STEP = 4

Z_GROUPS = [[y * ZL + z for z in range(ZL)] for y in range(Y)]
X_GROUPS = [
    [(x * ZH + z) * CORES + c for x in range(X)] for z in range(ZH) for c in range(CORES)
]
H_GROUPS = [
    [(x * ZH + z) * CORES + c for z in range(ZH)] for x in range(X) for c in range(CORES)
]
SWAP = [(d, d ^ 1) for d in range(X * ZH * CORES)]


def y_shift(step):
    return [
        (y * ZL + z, (y + step) % Y * ZL + z) for y in range(Y) for z in range(ZL)
    ]


UP, DOWN = y_shift(1), y_shift(-1)
PIECE_AT = (0, 4, 8, 12, 16, 18, 20, 24, 28)
PIECE_LEN = (4, 4, 4, 4, 2, 2, 4, 4, 4)
LIVE = Y * ZL


def sum_kernel(parity, slots, weights, *refs):
    pieces = refs[: len(PIECE_AT)]
    out, blocks, sems = refs[len(PIECE_AT) :]
    step = pl.program_id(0)

    @pl.when(step == 0)
    def _():
        copies = [
            pltpu.make_async_copy(piece, blocks.at[pl.ds(at, count)], sems.at[i])
            for i, (piece, at, count) in enumerate(zip(pieces, PIECE_AT, PIECE_LEN))
        ]
        for copy in copies:
            copy.start()
        blocks[LIVE] = jnp.zeros(blocks.shape[1:], blocks.dtype)
        for copy in copies:
            copy.wait()

    depth = weights.shape[2]
    for q in range(STEP):
        base = ((step * STEP + q) * CORES + parity[0]) * depth
        total = None
        for t in range(0, depth, 2):
            group = range(t, min(t + 2, depth))
            left = jnp.concatenate([weights[q, 0, u] for u in group], axis=1)
            right = jnp.concatenate([blocks[slots[base + u]] for u in group], axis=0)
            term = jnp.dot(left, right, preferred_element_type=jnp.float32)
            total = term if total is None else total + term
        out[q] = total.astype(out.dtype)


def partial_sums(parity, slots, weights, pieces, dtype):
    _, _, depth, size, _ = weights.shape
    classes = pieces[0].shape[-1]
    grid_spec = pltpu.PrefetchScalarGridSpec(
        num_scalar_prefetch=2,
        grid=(PAIRS // STEP,),
        in_specs=[
            pl.BlockSpec(
                (STEP, 1, depth, size, size), lambda i, parity, slots: (i, parity[0], 0, 0, 0)
            )
        ]
        + [pl.BlockSpec(memory_space=pl.ANY)] * len(pieces),
        out_specs=pl.BlockSpec((STEP, size, classes), lambda i, parity, slots: (i, 0, 0)),
        scratch_shapes=[
            pltpu.VMEM((LIVE + 1, size, classes), jnp.bfloat16),
            pltpu.SemaphoreType.DMA((len(pieces),)),
        ],
    )
    return pl.pallas_call(
        sum_kernel,
        grid_spec=grid_spec,
        out_shape=jax.ShapeDtypeStruct((PAIRS, size, classes), dtype),
        compiler_params=pltpu.CompilerParams(vmem_limit_bytes=32 * 1024 * 1024),
        cost_estimate=pl.CostEstimate(
            flops=2 * PAIRS * depth * size * size * classes,
            bytes_accessed=6 * 1024 * 1024,
            transcendentals=0,
        ),
    )(parity, slots, weights, *pieces)


def gather_blocks(outgoing):
    spread = jnp.broadcast_to(outgoing[None], (ZL,) + outgoing.shape)
    own = lax.all_to_all(spread, "src", 0, 0, axis_index_groups=Z_GROUPS)
    up, down = [own], [own]
    for _ in range(3):
        up.append(lax.ppermute(up[-1], "src", UP))
        down.append(lax.ppermute(down[-1], "src", DOWN))
    far_up = lax.ppermute(up[3][:2], "src", UP)
    far_down = lax.ppermute(down[3][2:], "src", DOWN)
    return [own, down[1], down[2], down[3], far_up, far_down, up[3], up[2], up[1]]


def per_device(prior, degrees, seed_mask, seed_labels, adjacency, block_cols, slot_counts):
    classes = prior.shape[1]
    depth, size = adjacency.shape[3], adjacency.shape[4]
    weights = adjacency.reshape(PAIRS, CORES, depth, size, size)
    core = lax.axis_index("dst") % CORES
    mine = core.astype(jnp.int32).reshape(1)
    other = 1 - mine
    y = lax.axis_index("src") // ZL
    columns = block_cols[0, 0]
    relative = (columns // ZL - y) % Y * ZL + columns % ZL
    active = jnp.arange(depth, dtype=jnp.int32)[None, :] < slot_counts[0, 0][:, None]
    slots = jnp.where(active, relative, LIVE).astype(jnp.int32).reshape(-1)
    inverse_root = lax.rsqrt(degrees.astype(jnp.float32))[:, None]
    onehot = (seed_labels[:, None] == jnp.arange(classes, dtype=jnp.int32)[None, :]).astype(
        jnp.float32
    )
    seeded = seed_mask[:, None] > 0
    scores = prior
    for _ in range(SWEEPS):
        outgoing = (inverse_root * scores).astype(jnp.bfloat16)
        pieces = gather_blocks(outgoing)
        send = partial_sums(other, slots, weights, pieces, jnp.bfloat16)
        swapped = lax.ppermute(send, "dst", SWAP)
        keep = partial_sums(mine, slots, weights, pieces, jnp.float32)
        chip = (keep + swapped.astype(jnp.float32)).astype(jnp.bfloat16)
        chip = chip.reshape(X, ZH, size, classes)
        rows = lax.all_to_all(chip, "dst", 0, 0, axis_index_groups=X_GROUPS)
        rows = jnp.sum(rows.astype(jnp.float32), axis=0).astype(jnp.bfloat16)
        parts = lax.all_to_all(rows, "dst", 0, 0, axis_index_groups=H_GROUPS)
        summed = jnp.sum(parts.astype(jnp.float32), axis=0)
        hidden = RETAIN * inverse_root * summed + (1.0 - RETAIN) * prior
        scores = jnp.where(seeded, onehot, hidden)
    return scores


def solution(mesh):
    in_specs = (
        P(("src", "dst"), None),
        P(("src", "dst")),
        P(("src", "dst")),
        P(("src", "dst")),
        P("src", "dst", None, None, None, None),
        P("src", "dst", None, None),
        P("src", "dst", None),
    )
    out_specs = P(("src", "dst"), None)
    return jax.shard_map(
        per_device, mesh=mesh, in_specs=in_specs, out_specs=out_specs, check_vma=False
    )
```

```python
import jax
import jax.numpy as jnp
from jax import lax
from jax.experimental import pallas as pl
from jax.experimental.pallas import tpu as pltpu
from jax.sharding import PartitionSpec as P

SWEEPS = 2
RETAIN = 0.8
VMEM_LIMIT = 56 * 1024 * 1024

Y, ZL, X, ZH, CORES = 8, 4, 4, 3, 2
LIVE = Y * ZL

Z_GROUPS = [[y * ZL + z for z in range(ZL)] for y in range(Y)]
H_GROUPS = [
    [(x * ZH + z) * CORES + c for z in range(ZH)] for x in range(X) for c in range(CORES)
]


def along_y(partner):
    return [(y * ZL + z, partner(y) * ZL + z) for y in range(Y) for z in range(ZL)]


def along_x(flip):
    rest = ZH * CORES
    return [(x * rest + i, (x ^ flip) * rest + i) for x in range(X) for i in range(rest)]


Y_EVEN = along_y(lambda y: y ^ 1)
Y_ODD = along_y(lambda y: (y - 1 if y % 2 == 0 else y + 1) % Y)
X_EVEN, X_ODD = along_x(1), along_x(3)
SWAP = [(d, d ^ 1) for d in range(X * ZH * CORES)]

PIECE_AT = (0, 4, 8, 12, 16, 18, 20, 24, 28)
PIECE_LEN = (4, 4, 4, 4, 2, 2, 4, 4, 4)


def sum_kernel(place, slots, weights, *refs):
    pieces = refs[: len(PIECE_AT)]
    out, blocks, sems = refs[len(PIECE_AT) :]
    step = pl.program_id(0)

    @pl.when(step == 0)
    def _():
        copies = [
            pltpu.make_async_copy(piece, blocks.at[pl.ds(at, count)], sems.at[i])
            for i, (piece, at, count) in enumerate(zip(pieces, PIECE_AT, PIECE_LEN))
        ]
        for copy in copies:
            copy.start()
        blocks[LIVE] = jnp.zeros(blocks.shape[1:], blocks.dtype)
        for copy in copies:
            copy.wait()

    depth = weights.shape[2]
    for q in range(ZH):
        base = (((step ^ place[0]) * ZH + q) * CORES + place[1]) * depth
        total = None
        for t in range(0, depth, 2):
            group = range(t, min(t + 2, depth))
            left = jnp.concatenate([weights[q, 0, u] for u in group], axis=1)
            right = jnp.concatenate([blocks[slots[base + u]] for u in group], axis=0)
            term = jnp.dot(left, right, preferred_element_type=jnp.float32)
            total = term if total is None else total + term
        out[0, q] = total.astype(out.dtype)


def partial_sums(place, slots, weights, pieces, dtype):
    _, _, depth, size, _ = weights.shape
    classes = pieces[0].shape[-1]
    grid_spec = pltpu.PrefetchScalarGridSpec(
        num_scalar_prefetch=2,
        grid=(X,),
        in_specs=[
            pl.BlockSpec(
                (ZH, 1, depth, size, size),
                lambda i, place, slots: (i ^ place[0], place[1], 0, 0, 0),
            )
        ]
        + [pl.BlockSpec(memory_space=pl.ANY)] * len(pieces),
        out_specs=pl.BlockSpec((1, ZH, size, classes), lambda i, place, slots: (i, 0, 0, 0)),
        scratch_shapes=[
            pltpu.VMEM((LIVE + 1, size, classes), jnp.bfloat16),
            pltpu.SemaphoreType.DMA((len(pieces),)),
        ],
    )
    return pl.pallas_call(
        sum_kernel,
        grid_spec=grid_spec,
        out_shape=jax.ShapeDtypeStruct((X, ZH, size, classes), dtype),
        compiler_params=pltpu.CompilerParams(vmem_limit_bytes=VMEM_LIMIT),
        cost_estimate=pl.CostEstimate(
            flops=2 * X * ZH * depth * size * size * classes,
            bytes_accessed=6 * 1024 * 1024,
            transcendentals=0,
        ),
    )(place, slots, weights, *pieces)


def gather_blocks(outgoing):
    spread = jnp.broadcast_to(outgoing[None], (ZL,) + outgoing.shape)
    own = lax.all_to_all(spread, "src", 0, 0, axis_index_groups=Z_GROUPS)
    even, odd = [own], [own]
    for _ in range(3):
        over_even = lax.ppermute(odd[-1], "src", Y_EVEN)
        over_odd = lax.ppermute(even[-1], "src", Y_ODD)
        even.append(over_even)
        odd.append(over_odd)
    half = ZL // 2
    far_even = lax.ppermute(odd[3][:half], "src", Y_EVEN)
    far_odd = lax.ppermute(even[3][half:], "src", Y_ODD)
    return [own, even[1], even[2], even[3], far_even, far_odd, odd[3], odd[2], odd[1]]


def reduce_over_x(chip):
    half = chip.shape[-1] // 2
    first, second = chip[..., :half], chip[..., half:]
    wire = jnp.bfloat16
    near_a = lax.ppermute(first[1:3].astype(wire), "dst", X_EVEN)
    near_b = lax.ppermute(second[2:4].astype(wire), "dst", X_ODD)
    pass_a = (first[3] + near_a[1].astype(jnp.float32)).astype(wire)
    far_a = lax.ppermute(pass_a, "dst", X_ODD)
    pass_b = (second[1] + near_b[0].astype(jnp.float32)).astype(wire)
    far_b = lax.ppermute(pass_b, "dst", X_EVEN)
    whole_a = first[0] + near_a[0].astype(jnp.float32) + far_a.astype(jnp.float32)
    whole_b = second[0] + near_b[1].astype(jnp.float32) + far_b.astype(jnp.float32)
    return jnp.concatenate([whole_a, whole_b], axis=-1)


def per_device(prior, degrees, seed_mask, seed_labels, adjacency, block_cols, slot_counts):
    classes = prior.shape[1]
    depth, size = adjacency.shape[3], adjacency.shape[4]
    weights = adjacency.reshape(X * ZH, CORES, depth, size, size)
    dst = lax.axis_index("dst").astype(jnp.int32)
    x, core = dst // (ZH * CORES), dst % CORES
    mine = jnp.stack([x, core])
    other = jnp.stack([x, 1 - core])
    y = (lax.axis_index("src") // ZL).astype(jnp.int32)
    toward = 1 - 2 * (y % 2)
    columns = block_cols[0, 0]
    relative = ((columns // ZL - y) * toward + Y) % Y * ZL + columns % ZL
    active = jnp.arange(depth, dtype=jnp.int32)[None, :] < slot_counts[0, 0][:, None]
    slots = jnp.where(active, relative, LIVE).astype(jnp.int32).reshape(-1)
    inverse_root = lax.rsqrt(degrees.astype(jnp.float32))[:, None]
    onehot = (seed_labels[:, None] == jnp.arange(classes, dtype=jnp.int32)[None, :]).astype(
        jnp.float32
    )
    seeded = seed_mask[:, None] > 0
    scores = prior
    for _ in range(SWEEPS):
        outgoing = (inverse_root * scores).astype(jnp.bfloat16)
        pieces = gather_blocks(outgoing)
        send = partial_sums(other, slots, weights, pieces, jnp.bfloat16)
        swapped = lax.ppermute(send, "dst", SWAP)
        keep = partial_sums(mine, slots, weights, pieces, jnp.float32)
        chip = keep + swapped.astype(jnp.float32)
        rows = reduce_over_x(chip).astype(jnp.bfloat16)
        parts = lax.all_to_all(rows, "dst", 0, 0, axis_index_groups=H_GROUPS)
        summed = jnp.sum(parts.astype(jnp.float32), axis=0)
        hidden = RETAIN * inverse_root * summed + (1.0 - RETAIN) * prior
        scores = jnp.where(seeded, onehot, hidden)
    return scores


def solution(mesh):
    in_specs = (
        P(("src", "dst"), None),
        P(("src", "dst")),
        P(("src", "dst")),
        P(("src", "dst")),
        P("src", "dst", None, None, None, None),
        P("src", "dst", None, None),
        P("src", "dst", None),
    )
    out_specs = P(("src", "dst"), None)
    return jax.shard_map(
        per_device, mesh=mesh, in_specs=in_specs, out_specs=out_specs, check_vma=False
    )
```

```python
import jax
import jax.numpy as jnp
from jax import lax
from jax.experimental import pallas as pl
from jax.experimental.pallas import tpu as pltpu
from jax.sharding import PartitionSpec as P

SWEEPS = 2
RETAIN = 0.8

Y, ZL, X, ZH, CORES = 8, 4, 4, 3, 2
PAIRS = X * ZH
STEP = 4

Z_GROUPS = [[y * ZL + z for z in range(ZL)] for y in range(Y)]
X_GROUPS = [
    [(x * ZH + z) * CORES + c for x in range(X)] for z in range(ZH) for c in range(CORES)
]
H_GROUPS = [
    [(x * ZH + z) * CORES + c for z in range(ZH)] for x in range(X) for c in range(CORES)
]
SWAP = [(d, d ^ 1) for d in range(X * ZH * CORES)]


def along_y(step):
    rest = X * ZH * CORES
    pairs = []
    for y in range(Y):
        for z in range(ZL):
            for d in range(rest):
                there = (y + (step if d % CORES == 0 else -step)) % Y
                pairs.append(((y * ZL + z) * rest + d, (there * ZL + z) * rest + d))
    return pairs


ALONG, AGAINST = along_y(1), along_y(-1)
PIECE_AT = (0, 4, 8, 12, 16, 18, 20, 24, 28)
PIECE_LEN = (4, 4, 4, 4, 2, 2, 4, 4, 4)
LIVE = Y * ZL


def sum_kernel(parity, slots, weights, *refs):
    pieces = refs[: len(PIECE_AT)]
    out, blocks, sems = refs[len(PIECE_AT) :]
    step = pl.program_id(0)

    @pl.when(step == 0)
    def _():
        copies = [
            pltpu.make_async_copy(piece, blocks.at[pl.ds(at, count)], sems.at[i])
            for i, (piece, at, count) in enumerate(zip(pieces, PIECE_AT, PIECE_LEN))
        ]
        for copy in copies:
            copy.start()
        for copy in copies:
            copy.wait()

    depth = weights.shape[2]
    for q in range(STEP):
        base = ((step * STEP + q) * CORES + parity[0]) * depth
        total = None
        for t in range(0, depth, 2):
            group = range(t, min(t + 2, depth))
            left = jnp.concatenate([weights[q, 0, u] for u in group], axis=1)
            right = jnp.concatenate([blocks[slots[base + u]] for u in group], axis=0)
            term = jnp.dot(left, right, preferred_element_type=jnp.float32)
            total = term if total is None else total + term
        out[q] = total.astype(out.dtype)


def partial_sums(parity, slots, weights, pieces, dtype):
    _, _, depth, size, _ = weights.shape
    classes = pieces[0].shape[-1]
    grid_spec = pltpu.PrefetchScalarGridSpec(
        num_scalar_prefetch=2,
        grid=(PAIRS // STEP,),
        in_specs=[
            pl.BlockSpec(
                (STEP, 1, depth, size, size), lambda i, parity, slots: (i, parity[0], 0, 0, 0)
            )
        ]
        + [pl.BlockSpec(memory_space=pl.ANY)] * len(pieces),
        out_specs=pl.BlockSpec((STEP, size, classes), lambda i, parity, slots: (i, 0, 0)),
        scratch_shapes=[
            pltpu.VMEM((LIVE, size, classes), jnp.bfloat16),
            pltpu.SemaphoreType.DMA((len(pieces),)),
        ],
    )
    return pl.pallas_call(
        sum_kernel,
        grid_spec=grid_spec,
        out_shape=jax.ShapeDtypeStruct((PAIRS, size, classes), dtype),
        compiler_params=pltpu.CompilerParams(vmem_limit_bytes=32 * 1024 * 1024),
        cost_estimate=pl.CostEstimate(
            flops=2 * PAIRS * depth * size * size * classes,
            bytes_accessed=6 * 1024 * 1024,
            transcendentals=0,
        ),
    )(parity, slots, weights, *pieces)


def gather_blocks(outgoing):
    spread = jnp.broadcast_to(outgoing[None], (ZL,) + outgoing.shape)
    own = lax.all_to_all(spread, "src", 0, 0, axis_index_groups=Z_GROUPS)
    first, second = [own], [own]
    for _ in range(3):
        first.append(lax.ppermute(first[-1], ("src", "dst"), ALONG))
        second.append(lax.ppermute(second[-1], ("src", "dst"), AGAINST))
    half = ZL // 2
    far_first = lax.ppermute(first[3][:half], ("src", "dst"), ALONG)
    far_second = lax.ppermute(second[3][half:], ("src", "dst"), AGAINST)
    return [own, first[1], first[2], first[3], far_first, far_second, second[3], second[2], second[1]]


def per_device(prior, degrees, seed_mask, seed_labels, adjacency, block_cols, slot_counts):
    classes = prior.shape[1]
    depth, size = adjacency.shape[3], adjacency.shape[4]
    active = jnp.arange(depth, dtype=jnp.int32)[None, :] < slot_counts[0, 0][:, None]
    weights = jnp.where(active[:, :, None, None], adjacency[0, 0], jnp.zeros((), adjacency.dtype))
    weights = weights.reshape(PAIRS, CORES, depth, size, size)
    core = lax.axis_index("dst").astype(jnp.int32) % CORES
    mine = core.reshape(1)
    other = 1 - mine
    y = lax.axis_index("src").astype(jnp.int32) // ZL
    columns = block_cols[0, 0]
    away = (columns // ZL - y) * (2 * core - 1)
    slots = ((away + Y) % Y * ZL + columns % ZL).reshape(-1)
    inverse_root = lax.rsqrt(degrees.astype(jnp.float32))[:, None]
    onehot = (seed_labels[:, None] == jnp.arange(classes, dtype=jnp.int32)[None, :]).astype(
        jnp.float32
    )
    seeded = seed_mask[:, None] > 0
    scores = prior
    for _ in range(SWEEPS):
        outgoing = (inverse_root * scores).astype(jnp.bfloat16)
        pieces = gather_blocks(outgoing)
        send = partial_sums(other, slots, weights, pieces, jnp.bfloat16)
        swapped = lax.ppermute(send, "dst", SWAP)
        keep = partial_sums(mine, slots, weights, pieces, jnp.float32)
        chip = (keep + swapped.astype(jnp.float32)).astype(jnp.bfloat16)
        chip = chip.reshape(X, ZH, size, classes)
        rows = lax.all_to_all(chip, "dst", 0, 0, axis_index_groups=X_GROUPS)
        rows = jnp.sum(rows.astype(jnp.float32), axis=0).astype(jnp.bfloat16)
        parts = lax.all_to_all(rows, "dst", 0, 0, axis_index_groups=H_GROUPS)
        summed = jnp.sum(parts.astype(jnp.float32), axis=0)
        hidden = RETAIN * inverse_root * summed + (1.0 - RETAIN) * prior
        scores = jnp.where(seeded, onehot, hidden)
    return scores


def solution(mesh):
    in_specs = (
        P(("src", "dst"), None),
        P(("src", "dst")),
        P(("src", "dst")),
        P(("src", "dst")),
        P("src", "dst", None, None, None, None),
        P("src", "dst", None, None),
        P("src", "dst", None),
    )
    out_specs = P(("src", "dst"), None)
    return jax.shard_map(
        per_device, mesh=mesh, in_specs=in_specs, out_specs=out_specs, check_vma=False
    )
```

```python
import jax
import jax.numpy as jnp
from jax import lax
from jax.experimental import pallas as pl
from jax.experimental.pallas import tpu as pltpu
from jax.sharding import PartitionSpec as P

SWEEPS = 2
RETAIN = 0.8

Y, ZL, X, ZH, CORES = 8, 4, 4, 3, 2
PAIRS = X * ZH
STEP = 4

Z_GROUPS = [[y * ZL + z for z in range(ZL)] for y in range(Y)]
Y_GROUPS = [[y * ZL + z for y in range(Y)] for z in range(ZL)]
X_GROUPS = [
    [(x * ZH + z) * CORES + c for x in range(X)] for z in range(ZH) for c in range(CORES)
]
H_GROUPS = [
    [(x * ZH + z) * CORES + c for z in range(ZH)] for x in range(X) for c in range(CORES)
]
SWAP = [(d, d ^ 1) for d in range(X * ZH * CORES)]


def sum_kernel(parity, slots, weights, near, far, out):
    depth = weights.shape[2]
    for q in range(STEP):
        base = ((pl.program_id(0) * STEP + q) * CORES + parity[0]) * depth
        total = None
        for t in range(0, depth, 2):
            group = range(t, min(t + 2, depth))
            left = jnp.concatenate([weights[q, 0, u] for u in group], axis=1)
            rows = []
            for u in group:
                column = slots[base + u]
                y, z = column // ZL, column % ZL
                rows += [near[column], far[z * Y + y]]
            right = jnp.concatenate(rows, axis=0)
            term = jnp.dot(left, right, preferred_element_type=jnp.float32)
            total = term if total is None else total + term
        out[q] = total.astype(out.dtype)


def partial_sums(parity, slots, weights, near, far, dtype):
    _, _, depth, size, _ = weights.shape
    classes = near.shape[-1]
    whole = lambda i, parity, slots: (0, 0, 0)
    grid_spec = pltpu.PrefetchScalarGridSpec(
        num_scalar_prefetch=2,
        grid=(PAIRS // STEP,),
        in_specs=[
            pl.BlockSpec(
                (STEP, 1, depth, size, size), lambda i, parity, slots: (i, parity[0], 0, 0, 0)
            ),
            pl.BlockSpec(near.shape, whole),
            pl.BlockSpec(far.shape, whole),
        ],
        out_specs=pl.BlockSpec((STEP, size, classes), lambda i, parity, slots: (i, 0, 0)),
    )
    return pl.pallas_call(
        sum_kernel,
        grid_spec=grid_spec,
        out_shape=jax.ShapeDtypeStruct((PAIRS, size, classes), dtype),
        compiler_params=pltpu.CompilerParams(vmem_limit_bytes=32 * 1024 * 1024),
        cost_estimate=pl.CostEstimate(
            flops=2 * PAIRS * depth * size * size * classes,
            bytes_accessed=6 * 1024 * 1024,
            transcendentals=0,
        ),
    )(parity, slots, weights, near, far)


def spread(block, groups):
    count = len(groups[0])
    copies = jnp.broadcast_to(block[None], (count,) + block.shape)
    return lax.all_to_all(copies, "src", 0, 0, axis_index_groups=groups)


def per_device(prior, degrees, seed_mask, seed_labels, adjacency, block_cols, slot_counts):
    classes = prior.shape[1]
    depth, size = adjacency.shape[3], adjacency.shape[4]
    active = jnp.arange(depth, dtype=jnp.int32)[None, :] < slot_counts[0, 0][:, None]
    core = lax.axis_index("dst").astype(jnp.int32) % CORES
    mine = core.reshape(1)
    other = 1 - mine
    slots = block_cols[0, 0].reshape(-1)
    half = size // 2
    inverse_root = lax.rsqrt(degrees.astype(jnp.float32))[:, None]
    onehot = (seed_labels[:, None] == jnp.arange(classes, dtype=jnp.int32)[None, :]).astype(
        jnp.float32
    )
    seeded = seed_mask[:, None] > 0
    scores = prior
    for _ in range(SWEEPS):
        outgoing = (inverse_root * scores).astype(jnp.bfloat16)
        own = spread(outgoing[:half], Z_GROUPS)
        near = lax.all_gather(own, "src", axis_index_groups=Y_GROUPS)
        own, edges = lax.optimization_barrier((own, adjacency))
        ahead = own[0, 0, 0] > jnp.inf
        rest = jnp.where(ahead, jnp.zeros((), outgoing.dtype), outgoing[half:])
        far = spread(spread(rest, Y_GROUPS), Z_GROUPS)
        near = near.reshape(Y * ZL, half, classes)
        far = far.reshape(ZL * Y, half, classes)
        weights = jnp.where(active[:, :, None, None], edges[0, 0], jnp.zeros((), edges.dtype))
        weights = weights.reshape(PAIRS, CORES, depth, size, size)
        send = partial_sums(other, slots, weights, near, far, jnp.bfloat16)
        swapped = lax.ppermute(send, "dst", SWAP)
        keep = partial_sums(mine, slots, weights, near, far, jnp.float32)
        chip = (keep + swapped.astype(jnp.float32)).astype(jnp.bfloat16)
        chip = chip.reshape(X, ZH, size, classes)
        rows = lax.all_to_all(chip, "dst", 0, 0, axis_index_groups=X_GROUPS)
        rows = jnp.sum(rows.astype(jnp.float32), axis=0).astype(jnp.bfloat16)
        parts = lax.all_to_all(rows, "dst", 0, 0, axis_index_groups=H_GROUPS)
        summed = jnp.sum(parts.astype(jnp.float32), axis=0)
        hidden = RETAIN * inverse_root * summed + (1.0 - RETAIN) * prior
        scores = jnp.where(seeded, onehot, hidden)
    return scores


def solution(mesh):
    in_specs = (
        P(("src", "dst"), None),
        P(("src", "dst")),
        P(("src", "dst")),
        P(("src", "dst")),
        P("src", "dst", None, None, None, None),
        P("src", "dst", None, None),
        P("src", "dst", None),
    )
    out_specs = P(("src", "dst"), None)
    return jax.shard_map(
        per_device, mesh=mesh, in_specs=in_specs, out_specs=out_specs, check_vma=False
    )
```

```python
import jax
import jax.numpy as jnp
from jax import lax
from jax.experimental import pallas as pl
from jax.experimental.pallas import tpu as pltpu
from jax.sharding import PartitionSpec as P

SWEEPS = 2
RETAIN = 0.8

Y, ZL, X, ZH, CORES = 8, 4, 4, 3, 2
PAIRS = X * ZH
STEP = 4

Z_GROUPS = [[y * ZL + z for z in range(ZL)] for y in range(Y)]
X_GROUPS = [
    [(x * ZH + z) * CORES + c for x in range(X)] for z in range(ZH) for c in range(CORES)
]
H_GROUPS = [
    [(x * ZH + z) * CORES + c for z in range(ZH)] for x in range(X) for c in range(CORES)
]
SWAP = [(d, d ^ 1) for d in range(X * ZH * CORES)]


def y_shift(step):
    return [
        (y * ZL + z, (y + step) % Y * ZL + z) for y in range(Y) for z in range(ZL)
    ]


UP, DOWN = y_shift(1), y_shift(-1)
PIECE_AT = (0, 4, 8, 12, 16, 18, 20, 24, 28)
PIECE_LEN = (4, 4, 4, 4, 2, 2, 4, 4, 4)
LIVE = Y * ZL


def sum_kernel(parity, slots, weights, *refs):
    pieces = refs[: len(PIECE_AT)]
    out, blocks, sems = refs[len(PIECE_AT) :]
    step = pl.program_id(0)

    @pl.when(step == 0)
    def _():
        copies = [
            pltpu.make_async_copy(piece, blocks.at[pl.ds(at, count)], sems.at[i])
            for i, (piece, at, count) in enumerate(zip(pieces, PIECE_AT, PIECE_LEN))
        ]
        for copy in copies:
            copy.start()
        blocks[LIVE] = jnp.zeros(blocks.shape[1:], blocks.dtype)
        for copy in copies:
            copy.wait()

    depth = weights.shape[1]
    for q in range(STEP):
        base = ((step * STEP + q) * CORES + parity[0]) * depth
        total = None
        for t in range(0, depth, 2):
            group = range(t, min(t + 2, depth))
            left = jnp.concatenate([weights[q, u] for u in group], axis=1)
            right = jnp.concatenate([blocks[slots[base + u]] for u in group], axis=0)
            term = jnp.dot(left, right, preferred_element_type=jnp.float32)
            total = term if total is None else total + term
        out[q] = total.astype(out.dtype)


def partial_sums(parity, slots, weights, pieces, dtype):
    _, depth, size, _ = weights.shape
    classes = pieces[0].shape[-1]
    grid_spec = pltpu.PrefetchScalarGridSpec(
        num_scalar_prefetch=2,
        grid=(PAIRS // STEP,),
        in_specs=[
            pl.BlockSpec((STEP, depth, size, size), lambda i, parity, slots: (i, 0, 0, 0))
        ]
        + [pl.BlockSpec(memory_space=pl.ANY)] * len(pieces),
        out_specs=pl.BlockSpec((STEP, size, classes), lambda i, parity, slots: (i, 0, 0)),
        scratch_shapes=[
            pltpu.VMEM((LIVE + 1, size, classes), jnp.bfloat16),
            pltpu.SemaphoreType.DMA((len(pieces),)),
        ],
    )
    return pl.pallas_call(
        sum_kernel,
        grid_spec=grid_spec,
        out_shape=jax.ShapeDtypeStruct((PAIRS, size, classes), dtype),
        compiler_params=pltpu.CompilerParams(vmem_limit_bytes=32 * 1024 * 1024),
        cost_estimate=pl.CostEstimate(
            flops=2 * PAIRS * depth * size * size * classes,
            bytes_accessed=6 * 1024 * 1024,
            transcendentals=0,
        ),
    )(parity, slots, weights, *pieces)


def gather_blocks(outgoing):
    spread = jnp.broadcast_to(outgoing[None], (ZL,) + outgoing.shape)
    own = lax.all_to_all(spread, "src", 0, 0, axis_index_groups=Z_GROUPS)
    half = ZL // 2
    up2 = lax.ppermute(own, "src", y_shift(2))
    down2 = lax.ppermute(own, "src", y_shift(-2))
    up1 = lax.ppermute(own, "src", UP)
    down1 = lax.ppermute(own, "src", DOWN)
    up3 = lax.ppermute(up2, "src", UP)
    down3 = lax.ppermute(down2, "src", DOWN)
    far_up = lax.ppermute(up2[:half], "src", y_shift(2))
    far_down = lax.ppermute(down2[half:], "src", y_shift(-2))
    return [own, down1, down2, down3, far_up, far_down, up3, up2, up1]


def per_device(prior, degrees, seed_mask, seed_labels, adjacency, block_cols, slot_counts):
    classes = prior.shape[1]
    depth, size = adjacency.shape[3], adjacency.shape[4]
    weights = adjacency.reshape(PAIRS, CORES, depth, size, size)
    core = lax.axis_index("dst") % CORES
    here = lax.dynamic_index_in_dim(weights, core, 1, keepdims=False)
    away = lax.dynamic_index_in_dim(weights, 1 - core, 1, keepdims=False)
    mine = core.astype(jnp.int32).reshape(1)
    other = 1 - mine
    y = lax.axis_index("src") // ZL
    columns = block_cols[0, 0]
    relative = (columns // ZL - y) % Y * ZL + columns % ZL
    active = jnp.arange(depth, dtype=jnp.int32)[None, :] < slot_counts[0, 0][:, None]
    slots = jnp.where(active, relative, LIVE).astype(jnp.int32).reshape(-1)
    inverse_root = lax.rsqrt(degrees.astype(jnp.float32))[:, None]
    onehot = (seed_labels[:, None] == jnp.arange(classes, dtype=jnp.int32)[None, :]).astype(
        jnp.float32
    )
    seeded = seed_mask[:, None] > 0
    scores = prior
    for _ in range(SWEEPS):
        outgoing = (inverse_root * scores).astype(jnp.bfloat16)
        pieces = gather_blocks(outgoing)
        send = partial_sums(other, slots, away, pieces, jnp.bfloat16)
        swapped = lax.ppermute(send, "dst", SWAP)
        keep = partial_sums(mine, slots, here, pieces, jnp.float32)
        chip = (keep + swapped.astype(jnp.float32)).astype(jnp.bfloat16)
        chip = chip.reshape(X, ZH, size, classes)
        rows = lax.all_to_all(chip, "dst", 0, 0, axis_index_groups=X_GROUPS)
        rows = jnp.sum(rows.astype(jnp.float32), axis=0).astype(jnp.bfloat16)
        parts = lax.all_to_all(rows, "dst", 0, 0, axis_index_groups=H_GROUPS)
        summed = jnp.sum(parts.astype(jnp.float32), axis=0)
        hidden = RETAIN * inverse_root * summed + (1.0 - RETAIN) * prior
        scores = jnp.where(seeded, onehot, hidden)
    return scores


def solution(mesh):
    in_specs = (
        P(("src", "dst"), None),
        P(("src", "dst")),
        P(("src", "dst")),
        P(("src", "dst")),
        P("src", "dst", None, None, None, None),
        P("src", "dst", None, None),
        P("src", "dst", None),
    )
    out_specs = P(("src", "dst"), None)
    return jax.shard_map(
        per_device, mesh=mesh, in_specs=in_specs, out_specs=out_specs, check_vma=False
    )
```
